32 devices in a mesh: groups: 2 (over y), sec: 4 (over z), mpo: 2 (over x), rep: 2 (over core).
Axes of the slice: x: 2, y: 2, z: 4, core: 2. Of those that a mesh axis runs over, the one named last changes fastest.
Arguments:
- wave: bfloat16 [16, 128, 16, 256], P(('groups', 'sec'), None, None, 'rep'), parts along dimension 0, may hold values from -6 to 6
- left_env: bfloat16 [16, 8, 128, 128], P(('groups', 'mpo'), 'sec'), parts along dimension 0, may hold values from -0.5 to 0.5
- right_env: bfloat16 [16, 8, 256, 256], P(('groups', 'mpo'), 'sec', 'rep'), parts along dimension 0, may hold values from -0.375 to 0.375
- phys_op: bfloat16 [16, 16, 16], P(('groups', 'mpo')), parts along dimension 0, may hold values from -0.5 to 0.5
- source: int32 [16, 8], P(('groups', 'mpo')), parts along dimension 0, may hold values from 0 to 7, each once within a row
- sector_rows: int32 [16], P('groups'), parts along dimension 0, may hold values from 64 to 128, as said below
Outputs:
- product: float32 [16, 128, 16, 256], P(('groups', 'sec'), None, 'mpo', 'rep'), parts along dimension 0
The draws below stay inside these ranges and needn't reach their ends.
There are 2 independent parts, one for each index of `groups`. The reference program is written for one: setup_inputs(seed, part) draws one part's arguments, and reference() takes and returns one part's arrays. A program takes and returns all parts, laid end to end along the dimension named above; each array names one. Nothing has to cross between parts.
Inputs may be any that keep to these rules, and one draw needn't show every extreme that they name: `source`: each row is a permutation of the 8 sectors. `sector_rows`: rows of a block at or beyond its sector's count are ignored; some sector is full.
All inputs are finite; a program needn't handle non-finite values.
Results may differ from the reference program's by a relative error of at most 0.005.
Values may be sent and summed in bfloat16 or wider, within the bound.
A program may use at most 64 MiB of HBM per device.

```python
import jax
import jax.numpy as jnp
from jax import lax

DL = 128
DR = 256
PHYS = 16
NS = 8
NW = 8


def draw_sector_rows(key, part):
    key = jax.random.fold_in(key, 7)
    first, second = jax.random.split(key)
    counts = jax.random.randint(first, (NS,), DL // 2, DL + 1)
    where_full = jax.random.randint(second, (), 0, NS)
    return counts.at[where_full].set(DL).astype(jnp.int32)


def levels(own_key, extent, shards, low, top_value):
    level, own = 1.0, jax.random.fold_in(own_key, 6)
    for dim, blocks in shards:
        steps = jnp.exp(jax.random.uniform(jax.random.fold_in(own, dim), (blocks,), jnp.float32, low / len(shards), top_value / len(shards)))
        level = level * jnp.repeat(steps, extent[dim] // blocks).reshape([-1 if axis == dim else 1 for axis in range(len(extent))])
    return level


def bell_draw(stream_key, extent, spread, most, pieces=(), kind=jnp.bfloat16):
    array = spread * jax.random.normal(stream_key, extent, jnp.float32)
    if pieces:
        array = array * levels(stream_key, extent, pieces, -0.22, 0.18)
    return jnp.clip(array, -most, most).astype(kind)


def setup_inputs(seed: int = 0, part: int = 0) -> dict:
    key_list = jax.random.split(jax.random.key(seed), 7)
    own_keys = jax.random.split(jax.random.fold_in(key_list[6], part), 7)
    wave = bell_draw(own_keys[0], (NS, DL, PHYS, DR), 1.0, 6.0, ((0, 4), (3, 2)))
    left_env = bell_draw(own_keys[1], (NW, NS, DL, DL), DL ** -0.5, 0.5, ((0, 2), (1, 4)))
    right_env = bell_draw(own_keys[2], (NW, NS, DR, DR), DR ** -0.5, 0.375, ((0, 2), (1, 4), (2, 2)))
    phys_op = bell_draw(own_keys[3], (NW, PHYS, PHYS), (PHYS * NW) ** -0.5, 0.5, ((0, 2),))
    source = jax.vmap(lambda own: jax.random.permutation(own, NS))(jax.random.split(own_keys[4], NW)).reshape((NW, NS)).astype(jnp.int32)
    sector_rows = draw_sector_rows(jax.random.fold_in(jax.random.fold_in(key_list[6], part), 71), part)
    return {"wave": wave, "left_env": left_env, "right_env": right_env, "phys_op": phys_op, "source": source, "sector_rows": sector_rows}


def reference(wave, left_env, right_env, phys_op, source, sector_rows):
    rows = jnp.arange(DL, dtype=jnp.int32)
    keep = rows[None, :] < sector_rows[:, None]
    masked = jnp.where(keep[:, :, None, None], wave, jnp.zeros_like(wave))
    masked_f = masked.astype(jnp.float32)

    def one_term(total, term):
        op_w = phys_op[term].astype(jnp.float32)
        phys = jnp.einsum('alpr,qp->alrq', masked_f, op_w).astype(jnp.bfloat16)
        right = jnp.einsum('alrq,asr->alsq', phys.astype(jnp.float32), right_env[term].astype(jnp.float32)).astype(jnp.bfloat16)
        moved = jnp.einsum('aml,alsq->amsq', left_env[term].astype(jnp.float32), right.astype(jnp.float32)).astype(jnp.bfloat16)
        picked = jnp.take(moved, source[term], axis=0).astype(jnp.float32)
        return total + picked, None

    start = jnp.zeros((NS, DL, DR, PHYS), jnp.float32)
    total, unused = lax.scan(one_term, start, jnp.arange(NW, dtype=jnp.int32))
    product = jnp.transpose(total, (0, 1, 3, 2))
    return jnp.where(keep[:, :, None, None], product, jnp.zeros_like(product))
```

```python
import functools

import jax
import jax.numpy as jnp
from jax import lax
from jax.experimental import pallas as pl
from jax.experimental.pallas import tpu as pltpu
from jax.sharding import PartitionSpec as P

MESH = pl.DeviceIdType.MESH
GROUP = 16


def signal(sem, where):
    pl.semaphore_signal(sem, inc=1, device_id=where, device_id_type=MESH)


def kernel(
    sec_count, mpo_count, q_here,
    source_ref, rows_ref, wave_ref, left_ref, right_ref, op_ref,
    out_ref,
    wbuf, lbuf, rbuf, ph, rt, acc, sendbuf, from_left, from_right,
    wave_sems, left_sems, right_sems, send_sems, fl_sems, fr_sems, local_sems,
):
    sec = lax.axis_index("sec")
    mpo = lax.axis_index("mpo")
    rep = lax.axis_index("rep")
    sectors, dl = left_ref.shape[1], left_ref.shape[2]
    local_terms = left_ref.shape[0]
    terms = local_terms * mpo_count
    cols = right_ref.shape[2]
    depth = wbuf.shape[2] // dl

    barrier = pltpu.get_barrier_semaphore()
    signal(barrier, {"rep": 1 - rep})
    for step in range(1, mpo_count):
        signal(barrier, {"mpo": lax.rem(mpo + step, mpo_count)})

    @pl.when(sec > 0)
    def _():
        signal(barrier, {"sec": sec - 1})

    @pl.when(sec < sec_count - 1)
    def _():
        signal(barrier, {"sec": sec + 1})

    neighbours = (sec > 0).astype(jnp.int32) + (sec < sec_count - 1).astype(jnp.int32)
    pl.semaphore_wait(barrier, mpo_count + neighbours)

    wave_copy = pltpu.make_async_remote_copy(
        src_ref=wave_ref, dst_ref=wbuf.at[rep],
        send_sem=wave_sems.at[0], recv_sem=wave_sems.at[1],
        device_id={"rep": 1 - rep}, device_id_type=MESH,
    )
    wave_copy.start()
    env_copies = []
    for step in range(1, mpo_count):
        peer = {"mpo": lax.rem(mpo + step, mpo_count)}
        for ref, buf, sems in ((left_ref, lbuf, left_sems), (right_ref, rbuf, right_sems)):
            copy = pltpu.make_async_remote_copy(
                src_ref=ref, dst_ref=buf.at[mpo],
                send_sem=sems.at[0, step], recv_sem=sems.at[1, step],
                device_id=peer, device_id_type=MESH,
            )
            copy.start()
            env_copies.append(copy)
    own_wave = pltpu.make_async_copy(wave_ref, wbuf.at[rep], local_sems.at[0])
    own_left = pltpu.make_async_copy(left_ref, lbuf.at[mpo], local_sems.at[1])
    own_right = pltpu.make_async_copy(right_ref, rbuf.at[mpo], local_sems.at[2])
    own_wave.start()
    own_left.start()
    own_right.start()
    own_wave.wait()
    wave_copy.wait()

    def transform(part, group):
        rows = pl.ds(pl.multiple_of(group * (GROUP * depth), GROUP * depth), GROUP * depth)
        both = jnp.concatenate([wbuf[0, part, rows, :], wbuf[1, part, rows, :]], axis=1)
        result = jnp.dot(op_ref[...], both, preferred_element_type=jnp.float32)
        l_rows = pl.ds(pl.multiple_of(group * GROUP, GROUP), GROUP)
        ph[part, :, l_rows, :] = result.astype(jnp.bfloat16).reshape(
            terms * q_here, GROUP, 2 * cols
        )

    for part in range(sectors):
        @pl.loop(0, dl // GROUP)
        def _(group):
            transform(part, group)

    row_index = lax.broadcasted_iota(jnp.int32, (dl, cols), 0)

    def contract(owner):
        for part in range(sectors):
            live = row_index < rows_ref[sec * sectors + part]

            @pl.loop(0, local_terms)
            def _(term):
                whole_term = owner * local_terms + term
                states = ph[part, pl.ds(whole_term * q_here, q_here)]
                result = lax.dot_general(
                    states.reshape(q_here * dl, 2 * cols),
                    rbuf[owner, term, part],
                    (((1,), (1,)), ((), ())),
                    preferred_element_type=jnp.float32,
                )
                for q in range(q_here):
                    piece = jnp.where(live, result[q * dl:(q + 1) * dl], 0.0)
                    rt[whole_term, part, :, q * cols:(q + 1) * cols] = piece.astype(jnp.bfloat16)

    own_right.wait()
    contract(mpo)
    for copy in env_copies:
        copy.wait()
    own_left.wait()
    for step in range(1, mpo_count):
        contract(lax.rem(mpo + step, mpo_count))

    width = q_here * cols
    tile = 256

    def partial(target):
        lefts, places = [], []
        for term in range(terms):
            src = source_ref[term, target] - sec * sectors
            inside = jnp.logical_and(src >= 0, src < sectors)
            place = jnp.clip(src, 0, sectors - 1)
            gate = jnp.where(inside, 1.0, 0.0)
            block = lbuf[term // local_terms, term % local_terms, place]
            lefts.append((block.astype(jnp.float32) * gate).astype(jnp.bfloat16))
            places.append(place)
        lhs = jnp.concatenate(lefts, axis=1)
        for n in range(0, width, tile):
            rhs = jnp.concatenate(
                [rt[term, places[term], :, n:n + tile] for term in range(terms)], axis=0
            )
            acc[:, n:n + tile] = jnp.dot(lhs, rhs, preferred_element_type=jnp.float32)

    def hop(owner, part, landing, sems, to):
        return pltpu.make_async_remote_copy(
            src_ref=sendbuf.at[owner, part], dst_ref=landing.at[owner, part],
            send_sem=send_sems.at[owner, part], recv_sem=sems.at[owner, part],
            device_id={"sec": to}, device_id_type=MESH,
        )

    def pass_on(owner, part, inner, landing, sems, to):
        partial(owner * sectors + part)

        @pl.when(inner)
        def _():
            hop(owner, part, landing, sems, to).wait_recv()
            acc[...] += landing[owner, part].astype(jnp.float32)

        sendbuf[owner, part] = acc[...].astype(jnp.bfloat16)
        hop(owner, part, landing, sems, to).start()

    up = lax.rem(sec + 1, sec_count)
    down = lax.rem(sec + sec_count - 1, sec_count)

    @pl.loop(0, sec_count - 1)
    def _(step):
        above = sec + sec_count - 1 - step
        below = step - (sec_count - 1) + sec

        @pl.when(above < sec_count)
        def _():
            @pl.loop(0, sectors)
            def _(part):
                pass_on(above, part, sec > 0, from_left, fl_sems, up)

        @pl.when(below >= 0)
        def _():
            @pl.loop(0, sectors)
            def _(part):
                pass_on(below, part, sec < sec_count - 1, from_right, fr_sems, down)

    for part in range(sectors):
        partial(sec * sectors + part)

        @pl.when(sec > 0)
        def _():
            hop(sec, part, from_left, fl_sems, up).wait_recv()
            acc[...] += from_left[sec, part].astype(jnp.float32)

        @pl.when(sec < sec_count - 1)
        def _():
            hop(sec, part, from_right, fr_sems, down).wait_recv()
            acc[...] += from_right[sec, part].astype(jnp.float32)

        live = row_index < rows_ref[sec * sectors + part]
        for q in range(q_here):
            columns = slice(q * cols, (q + 1) * cols)
            out_ref[part, :, columns] = jnp.where(live, acc[:, columns], 0.0)

    @pl.loop(0, sec_count)
    def _(owner):
        @pl.when(owner != sec)
        def _():
            for part in range(sectors):
                hop(owner, part, from_left, fl_sems, up).wait_send()


def per_device(sec_count, mpo_count, wave, left_env, right_env, phys_op, source, sector_rows):
    sectors, dl, phys_all, cols = wave.shape
    local_terms = phys_op.shape[0]
    terms = local_terms * mpo_count
    q_here = phys_all // mpo_count
    mpo = lax.axis_index("mpo")
    small = jnp.concatenate(
        [phys_op.reshape(local_terms, -1), source.astype(jnp.bfloat16)], axis=1
    )
    small = lax.all_gather(small, "mpo", axis=0, tiled=True)
    ops = small[:, :phys_all * phys_all].reshape(terms, phys_all, phys_all)
    order = small[:, phys_all * phys_all:].astype(jnp.int32)
    ops = lax.dynamic_slice_in_dim(ops, mpo * q_here, q_here, axis=1)
    same = jnp.eye(GROUP, dtype=jnp.bfloat16)
    spread = (ops[:, :, None, None, :] * same[None, None, :, :, None]).reshape(
        terms * q_here * GROUP, GROUP * phys_all
    )
    vmem = pl.BlockSpec(memory_space=pltpu.VMEM)
    smem = pl.BlockSpec(memory_space=pltpu.SMEM)
    width = q_here * cols
    bf16 = jnp.bfloat16
    out = pl.pallas_call(
        functools.partial(kernel, sec_count, mpo_count, q_here),
        out_shape=jax.ShapeDtypeStruct((sectors, dl, width), jnp.float32),
        in_specs=[smem, smem, vmem, vmem, vmem, vmem],
        out_specs=vmem,
        scratch_shapes=[
            pltpu.VMEM((2, sectors, dl * phys_all, cols), bf16),
            pltpu.VMEM((mpo_count,) + left_env.shape, bf16),
            pltpu.VMEM((mpo_count,) + right_env.shape, bf16),
            pltpu.VMEM((sectors, terms * q_here, dl, 2 * cols), bf16),
            pltpu.VMEM((terms, sectors, dl, width), bf16),
            pltpu.VMEM((dl, width), jnp.float32),
            pltpu.VMEM((sec_count, sectors, dl, width), bf16),
            pltpu.VMEM((sec_count, sectors, dl, width), bf16),
            pltpu.VMEM((sec_count, sectors, dl, width), bf16),
            pltpu.SemaphoreType.DMA((2,)),
            pltpu.SemaphoreType.DMA((2, mpo_count)),
            pltpu.SemaphoreType.DMA((2, mpo_count)),
            pltpu.SemaphoreType.DMA((sec_count, sectors)),
            pltpu.SemaphoreType.DMA((sec_count, sectors)),
            pltpu.SemaphoreType.DMA((sec_count, sectors)),
            pltpu.SemaphoreType.DMA((3,)),
        ],
        compiler_params=pltpu.CompilerParams(
            collective_id=0, has_side_effects=True, vmem_limit_bytes=56 * 1024 * 1024
        ),
        cost_estimate=pl.CostEstimate(
            flops=6 * 10**9, bytes_accessed=8 * 2**20, transcendentals=0
        ),
    )(
        order, sector_rows, wave.reshape(sectors, dl * phys_all, cols),
        left_env, right_env, spread,
    )
    return out.reshape(sectors, dl, q_here, cols)


def solution(mesh):
    placed = (
        P(("groups", "sec"), None, None, "rep"),
        P(("groups", "mpo"), "sec", None, None),
        P(("groups", "mpo"), "sec", "rep", None),
        P(("groups", "mpo"), None, None),
        P(("groups", "mpo"), None),
        P("groups"),
    )
    return jax.shard_map(
        functools.partial(per_device, mesh.shape["sec"], mesh.shape["mpo"]),
        mesh=mesh,
        in_specs=placed,
        out_specs=P(("groups", "sec"), None, "mpo", "rep"),
        check_vma=False,
    )
```

```python
import functools

import jax
import jax.numpy as jnp
from jax import lax
from jax.experimental import pallas as pl
from jax.experimental.pallas import tpu as pltpu
from jax.sharding import PartitionSpec as P

MESH = pl.DeviceIdType.MESH
GROUP = 16


def signal(sem, where):
    pl.semaphore_signal(sem, inc=1, device_id=where, device_id_type=MESH)


def kernel(
    sec_count, mpo_count, q_here,
    source_ref, rows_ref, wave_ref, left_ref, right_ref, phys_ref,
    out_ref,
    order_buf, order, pbuf, op_ref, wbuf, lbuf, rbuf, ph, rt, acc, sendbuf, from_left, from_right,
    wave_sems, small_sems, left_sems, right_sems, send_sems, fl_sems, fr_sems, local_sems, turn,
):
    sec = lax.axis_index("sec")
    mpo = lax.axis_index("mpo")
    rep = lax.axis_index("rep")
    sectors, dl = left_ref.shape[1], left_ref.shape[2]
    local_terms = left_ref.shape[0]
    terms = local_terms * mpo_count
    cols = right_ref.shape[2]
    depth = wbuf.shape[2] // dl

    barrier = pltpu.get_barrier_semaphore()
    signal(barrier, {"rep": 1 - rep})
    for step in range(1, mpo_count):
        signal(barrier, {"mpo": lax.rem(mpo + step, mpo_count)})

    @pl.when(sec > 0)
    def _():
        signal(barrier, {"sec": sec - 1})

    @pl.when(sec < sec_count - 1)
    def _():
        signal(barrier, {"sec": sec + 1})

    neighbours = (sec > 0).astype(jnp.int32) + (sec < sec_count - 1).astype(jnp.int32)
    pl.semaphore_wait(barrier, mpo_count + neighbours)

    wave_copy = pltpu.make_async_remote_copy(
        src_ref=wave_ref, dst_ref=wbuf.at[rep],
        send_sem=wave_sems.at[0], recv_sem=wave_sems.at[1],
        device_id={"rep": 1 - rep}, device_id_type=MESH,
    )

    def to_peers(ref, buf, sems):
        return [
            pltpu.make_async_remote_copy(
                src_ref=ref, dst_ref=buf.at[mpo],
                send_sem=sems.at[0, step], recv_sem=sems.at[1, step],
                device_id={"mpo": lax.rem(mpo + step, mpo_count)}, device_id_type=MESH,
            )
            for step in range(1, mpo_count)
        ]

    phys_copies = to_peers(phys_ref, pbuf, small_sems.at[0])
    order_copies = to_peers(source_ref, order_buf, small_sems.at[1])
    right_copies = to_peers(right_ref, rbuf, right_sems)
    left_copies = to_peers(left_ref, lbuf, left_sems)
    env_copies = right_copies + left_copies
    for copy in phys_copies + order_copies:
        copy.start()
    wave_copy.start()

    @pl.when(rep == 0)
    def _():
        for copy in env_copies:
            copy.start()

    own_wave = pltpu.make_async_copy(wave_ref, wbuf.at[rep], local_sems.at[0])
    own_left = pltpu.make_async_copy(left_ref, lbuf.at[mpo], local_sems.at[1])
    own_right = pltpu.make_async_copy(right_ref, rbuf.at[mpo], local_sems.at[2])
    own_wave.start()
    own_left.start()
    own_right.start()
    pbuf[mpo] = phys_ref[...]
    order_buf[mpo] = source_ref[...]
    for copy in phys_copies + order_copies:
        copy.wait()
    to_scalars = pltpu.make_async_copy(order_buf, order, local_sems.at[3])
    to_scalars.start()
    phys_all = phys_ref.shape[1]
    spread_rows, spread_cols = op_ref.shape
    flat = pbuf[...].reshape(terms * phys_all, phys_all)
    r = lax.broadcasted_iota(jnp.int32, (spread_rows, terms * phys_all), 0) // GROUP
    c = lax.broadcasted_iota(jnp.int32, (spread_rows, terms * phys_all), 1)
    want = (r // q_here) * phys_all + mpo * q_here + r % q_here
    pick = jnp.where(want == c, 1.0, 0.0).astype(jnp.bfloat16)
    tall = jnp.dot(pick, flat, preferred_element_type=jnp.float32).astype(jnp.bfloat16)
    p = lax.broadcasted_iota(jnp.int32, (phys_all, spread_cols), 0)
    c = lax.broadcasted_iota(jnp.int32, (phys_all, spread_cols), 1)
    repeat = jnp.where(c % phys_all == p, 1.0, 0.0).astype(jnp.bfloat16)
    wide = jnp.dot(tall, repeat, preferred_element_type=jnp.float32)
    r = lax.broadcasted_iota(jnp.int32, (spread_rows, spread_cols), 0)
    c = lax.broadcasted_iota(jnp.int32, (spread_rows, spread_cols), 1)
    op_ref[...] = jnp.where(r % GROUP == c // phys_all, wide, 0.0).astype(jnp.bfloat16)
    own_wave.wait()
    wave_copy.wait()

    def transform(part, group):
        rows = pl.ds(pl.multiple_of(group * (GROUP * depth), GROUP * depth), GROUP * depth)
        both = jnp.concatenate([wbuf[0, part, rows, :], wbuf[1, part, rows, :]], axis=1)
        result = jnp.dot(op_ref[...], both, preferred_element_type=jnp.float32)
        l_rows = pl.ds(pl.multiple_of(group * GROUP, GROUP), GROUP)
        ph[part, :, l_rows, :] = result.astype(jnp.bfloat16).reshape(
            terms * q_here, GROUP, 2 * cols
        )

    for part in range(sectors):
        @pl.loop(0, dl // GROUP)
        def _(group):
            transform(part, group)

    row_index = lax.broadcasted_iota(jnp.int32, (dl, cols), 0)

    def contract(owner):
        for part in range(sectors):
            live = row_index < rows_ref[sec * sectors + part]

            @pl.loop(0, local_terms)
            def _(term):
                whole_term = owner * local_terms + term
                states = ph[part, pl.ds(whole_term * q_here, q_here)]
                result = lax.dot_general(
                    states.reshape(q_here * dl, 2 * cols),
                    rbuf[owner, term, part],
                    (((1,), (1,)), ((), ())),
                    preferred_element_type=jnp.float32,
                )
                for q in range(q_here):
                    piece = jnp.where(live, result[q * dl:(q + 1) * dl], 0.0)
                    rt[whole_term, part, :, q * cols:(q + 1) * cols] = piece.astype(jnp.bfloat16)

    own_right.wait()
    contract(mpo)

    @pl.when(rep == 0)
    def _():
        for copy in env_copies:
            copy.wait_send()
        signal(turn, {"rep": 1})

    @pl.when(rep == 1)
    def _():
        pl.semaphore_wait(turn, 1)
        for copy in env_copies:
            copy.start()

    for step in range(1, mpo_count):
        right_copies[step - 1].wait_recv()
        contract(lax.rem(mpo + mpo_count - step, mpo_count))
    own_left.wait()
    to_scalars.wait()
    for copy in left_copies:
        copy.wait_recv()

    width = q_here * cols
    tile = 256

    def partial(target):
        lefts, places = [], []
        for term in range(terms):
            src = order[term // local_terms, term % local_terms, target] - sec * sectors
            inside = jnp.logical_and(src >= 0, src < sectors)
            place = jnp.clip(src, 0, sectors - 1)
            gate = jnp.where(inside, 1.0, 0.0)
            block = lbuf[term // local_terms, term % local_terms, place]
            lefts.append((block.astype(jnp.float32) * gate).astype(jnp.bfloat16))
            places.append(place)
        lhs = jnp.concatenate(lefts, axis=1)
        for n in range(0, width, tile):
            rhs = jnp.concatenate(
                [rt[term, places[term], :, n:n + tile] for term in range(terms)], axis=0
            )
            acc[:, n:n + tile] = jnp.dot(lhs, rhs, preferred_element_type=jnp.float32)

    def hop(owner, part, landing, sems, to):
        return pltpu.make_async_remote_copy(
            src_ref=sendbuf.at[owner, part], dst_ref=landing.at[owner, part],
            send_sem=send_sems.at[owner, part], recv_sem=sems.at[owner, part],
            device_id={"sec": to}, device_id_type=MESH,
        )

    def pass_on(owner, part, inner, landing, sems, to):
        partial(owner * sectors + part)

        @pl.when(inner)
        def _():
            hop(owner, part, landing, sems, to).wait_recv()
            acc[...] += landing[owner, part].astype(jnp.float32)

        sendbuf[owner, part] = acc[...].astype(jnp.bfloat16)
        hop(owner, part, landing, sems, to).start()

    up = lax.rem(sec + 1, sec_count)
    down = lax.rem(sec + sec_count - 1, sec_count)

    @pl.loop(0, sec_count - 1)
    def _(step):
        above = sec + sec_count - 1 - step
        below = step - (sec_count - 1) + sec

        @pl.when(above < sec_count)
        def _():
            @pl.loop(0, sectors)
            def _(part):
                pass_on(above, part, sec > 0, from_left, fl_sems, up)

        @pl.when(below >= 0)
        def _():
            @pl.loop(0, sectors)
            def _(part):
                pass_on(below, part, sec < sec_count - 1, from_right, fr_sems, down)

    for part in range(sectors):
        partial(sec * sectors + part)

        @pl.when(sec > 0)
        def _():
            hop(sec, part, from_left, fl_sems, up).wait_recv()
            acc[...] += from_left[sec, part].astype(jnp.float32)

        @pl.when(sec < sec_count - 1)
        def _():
            hop(sec, part, from_right, fr_sems, down).wait_recv()
            acc[...] += from_right[sec, part].astype(jnp.float32)

        live = row_index < rows_ref[sec * sectors + part]
        for q in range(q_here):
            columns = slice(q * cols, (q + 1) * cols)
            out_ref[part, :, columns] = jnp.where(live, acc[:, columns], 0.0)

    @pl.loop(0, sec_count)
    def _(owner):
        @pl.when(owner != sec)
        def _():
            for part in range(sectors):
                hop(owner, part, from_left, fl_sems, up).wait_send()

    @pl.when(rep == 1)
    def _():
        for copy in env_copies:
            copy.wait_send()


def per_device(sec_count, mpo_count, wave, left_env, right_env, phys_op, source, sector_rows):
    sectors, dl, phys_all, cols = wave.shape
    local_terms = phys_op.shape[0]
    terms = local_terms * mpo_count
    q_here = phys_all // mpo_count
    vmem = pl.BlockSpec(memory_space=pltpu.VMEM)
    smem = pl.BlockSpec(memory_space=pltpu.SMEM)
    width = q_here * cols
    bf16 = jnp.bfloat16
    out = pl.pallas_call(
        functools.partial(kernel, sec_count, mpo_count, q_here),
        out_shape=jax.ShapeDtypeStruct((sectors, dl, width), jnp.float32),
        in_specs=[vmem, smem, vmem, vmem, vmem, vmem],
        out_specs=vmem,
        scratch_shapes=[
            pltpu.VMEM((mpo_count,) + source.shape, jnp.int32),
            pltpu.SMEM((mpo_count,) + source.shape, jnp.int32),
            pltpu.VMEM((mpo_count,) + phys_op.shape, bf16),
            pltpu.VMEM((terms * q_here * GROUP, GROUP * phys_all), bf16),
            pltpu.VMEM((2, sectors, dl * phys_all, cols), bf16),
            pltpu.VMEM((mpo_count,) + left_env.shape, bf16),
            pltpu.VMEM((mpo_count,) + right_env.shape, bf16),
            pltpu.VMEM((sectors, terms * q_here, dl, 2 * cols), bf16),
            pltpu.VMEM((terms, sectors, dl, width), bf16),
            pltpu.VMEM((dl, width), jnp.float32),
            pltpu.VMEM((sec_count, sectors, dl, width), bf16),
            pltpu.VMEM((sec_count, sectors, dl, width), bf16),
            pltpu.VMEM((sec_count, sectors, dl, width), bf16),
            pltpu.SemaphoreType.DMA((2,)),
            pltpu.SemaphoreType.DMA((2, 2, mpo_count)),
            pltpu.SemaphoreType.DMA((2, mpo_count)),
            pltpu.SemaphoreType.DMA((2, mpo_count)),
            pltpu.SemaphoreType.DMA((sec_count, sectors)),
            pltpu.SemaphoreType.DMA((sec_count, sectors)),
            pltpu.SemaphoreType.DMA((sec_count, sectors)),
            pltpu.SemaphoreType.DMA((4,)),
            pltpu.SemaphoreType.REGULAR,
        ],
        compiler_params=pltpu.CompilerParams(
            collective_id=0, has_side_effects=True, vmem_limit_bytes=56 * 1024 * 1024
        ),
        cost_estimate=pl.CostEstimate(
            flops=6 * 10**9, bytes_accessed=8 * 2**20, transcendentals=0
        ),
    )(
        source, sector_rows, wave.reshape(sectors, dl * phys_all, cols),
        left_env, right_env, phys_op,
    )
    return out.reshape(sectors, dl, q_here, cols)


def solution(mesh):
    placed = (
        P(("groups", "sec"), None, None, "rep"),
        P(("groups", "mpo"), "sec", None, None),
        P(("groups", "mpo"), "sec", "rep", None),
        P(("groups", "mpo"), None, None),
        P(("groups", "mpo"), None),
        P("groups"),
    )
    return jax.shard_map(
        functools.partial(per_device, mesh.shape["sec"], mesh.shape["mpo"]),
        mesh=mesh,
        in_specs=placed,
        out_specs=P(("groups", "sec"), None, "mpo", "rep"),
        check_vma=False,
    )
```

```python
import functools

import jax
import jax.numpy as jnp
from jax import lax
from jax.experimental import pallas as pl
from jax.experimental.pallas import tpu as pltpu
from jax.sharding import PartitionSpec as P

MESH = pl.DeviceIdType.MESH
GROUP = 16


def split(value, size):
    if size & (size - 1):
        return value // size, value % size
    return lax.shift_right_logical(value, size.bit_length() - 1), value & (size - 1)


def signal(sem, where):
    pl.semaphore_signal(sem, inc=1, device_id=where, device_id_type=MESH)


def kernel(
    sec_count, mpo_count, q_here,
    source_ref, rows_ref, wave_ref, left_ref, right_ref, phys_ref,
    out_ref,
    order_buf, order, pbuf, pick_ref, op_ref, wbuf, lbuf, rbuf, ph, rt, acc, sendbuf, from_left, from_right,
    wave_sems, small_sems, left_sems, right_sems, send_sems, fl_sems, fr_sems, local_sems, turn,
):
    sec = lax.axis_index("sec")
    mpo = lax.axis_index("mpo")
    rep = lax.axis_index("rep")
    sectors, dl = left_ref.shape[1], left_ref.shape[2]
    local_terms = left_ref.shape[0]
    terms = local_terms * mpo_count
    cols = right_ref.shape[2]
    depth = wbuf.shape[2] // dl
    chunks = rt.shape[0]
    q_chunk = q_here // chunks
    width = q_chunk * cols

    barrier = pltpu.get_barrier_semaphore()
    signal(barrier, {"rep": 1 - rep})
    for step in range(1, mpo_count):
        signal(barrier, {"mpo": lax.rem(mpo + step, mpo_count)})

    @pl.when(sec > 0)
    def _():
        signal(barrier, {"sec": sec - 1})

    @pl.when(sec < sec_count - 1)
    def _():
        signal(barrier, {"sec": sec + 1})

    phys_all = phys_ref.shape[1]
    spread_rows = op_ref.shape[0] * op_ref.shape[1]
    spread_cols = op_ref.shape[2]
    r = lax.broadcasted_iota(jnp.int32, (spread_rows, 1), 0)
    c = lax.broadcasted_iota(jnp.int32, (1, terms * phys_all), 1)
    r, lane = split(r, GROUP)
    r, q_in = split(r, q_chunk)
    chunk_of, term_of = split(r, terms)
    want = term_of * phys_all + mpo * q_here + chunk_of * q_chunk + q_in
    pick_ref[...] = jnp.where(want == c, 1.0, 0.0).astype(jnp.bfloat16)
    c = lax.broadcasted_iota(jnp.int32, (1, spread_cols), 1)
    mask = jnp.where(lane == split(c, phys_all)[0], 1.0, 0.0).astype(jnp.bfloat16)
    op_ref[...] = mask.reshape(op_ref.shape)
    neighbours = (sec > 0).astype(jnp.int32) + (sec < sec_count - 1).astype(jnp.int32)
    pl.semaphore_wait(barrier, mpo_count + neighbours)

    wave_copies = [
        pltpu.make_async_remote_copy(
            src_ref=wave_ref.at[part], dst_ref=wbuf.at[rep, part],
            send_sem=wave_sems.at[0, part], recv_sem=wave_sems.at[1, part],
            device_id={"rep": 1 - rep}, device_id_type=MESH,
        )
        for part in range(sectors)
    ]

    def to_peers(ref, buf, sems):
        return [
            pltpu.make_async_remote_copy(
                src_ref=ref, dst_ref=buf.at[mpo],
                send_sem=sems.at[0, step], recv_sem=sems.at[1, step],
                device_id={"mpo": lax.rem(mpo + step, mpo_count)}, device_id_type=MESH,
            )
            for step in range(1, mpo_count)
        ]

    phys_copies = to_peers(phys_ref, pbuf, small_sems.at[0])
    order_copies = to_peers(source_ref, order_buf, small_sems.at[1])
    right_copies = to_peers(right_ref, rbuf, right_sems)
    left_copies = to_peers(left_ref, lbuf, left_sems)
    env_copies = right_copies + left_copies
    for copy in phys_copies + order_copies:
        copy.start()
    for copy in wave_copies:
        copy.start()

    @pl.when(rep == 0)
    def _():
        for copy in env_copies:
            copy.start()

    own_wave = pltpu.make_async_copy(wave_ref, wbuf.at[rep], local_sems.at[0])
    own_left = pltpu.make_async_copy(left_ref, lbuf.at[mpo], local_sems.at[1])
    own_right = pltpu.make_async_copy(right_ref, rbuf.at[mpo], local_sems.at[2])
    own_wave.start()
    own_left.start()
    own_right.start()
    pbuf[mpo] = phys_ref[...]
    order_buf[mpo] = source_ref[...]
    for copy in phys_copies + order_copies:
        copy.wait()
    to_scalars = pltpu.make_async_copy(order_buf, order, local_sems.at[3])
    to_scalars.start()
    flat = pbuf[...].reshape(terms * phys_all, phys_all)
    tall = jnp.dot(pick_ref[...], flat, preferred_element_type=jnp.float32).astype(jnp.bfloat16)
    p = lax.broadcasted_iota(jnp.int32, (phys_all, spread_cols), 0)
    c = lax.broadcasted_iota(jnp.int32, (phys_all, spread_cols), 1)
    repeat = jnp.where(split(c, phys_all)[1] == p, 1.0, 0.0).astype(jnp.bfloat16)
    wide = jnp.dot(tall, repeat, preferred_element_type=jnp.float32).reshape(op_ref.shape)
    op_ref[...] = jnp.where(op_ref[...].astype(jnp.float32) > 0.5, wide, 0.0).astype(jnp.bfloat16)
    own_wave.wait()

    def transform(chunk, part):
        @pl.loop(0, dl // GROUP, unroll=2)
        def _(group):
            rows = pl.ds(pl.multiple_of(group * (GROUP * depth), GROUP * depth), GROUP * depth)
            both = jnp.concatenate([wbuf[0, part, rows, :], wbuf[1, part, rows, :]], axis=1)
            result = jnp.dot(op_ref[chunk], both, preferred_element_type=jnp.float32)
            l_rows = pl.ds(pl.multiple_of(group * GROUP, GROUP), GROUP)
            ph[part, :, l_rows, :] = result.astype(jnp.bfloat16).reshape(
                terms * q_chunk, GROUP, 2 * cols
            )

    row_index = lax.broadcasted_iota(jnp.int32, (dl, cols), 0)

    def contract(chunk, owner):
        for part in range(sectors):
            live = row_index < rows_ref[sec * sectors + part]

            @pl.loop(0, local_terms, unroll=2)
            def _(term):
                whole_term = owner * local_terms + term
                states = ph[part, pl.ds(whole_term * q_chunk, q_chunk)]
                result = lax.dot_general(
                    states.reshape(q_chunk * dl, 2 * cols),
                    rbuf[owner, term, part],
                    (((1,), (1,)), ((), ())),
                    preferred_element_type=jnp.float32,
                )
                for q in range(q_chunk):
                    piece = jnp.where(live, result[q * dl:(q + 1) * dl], 0.0)
                    rt[chunk, whole_term, part, :, q * cols:(q + 1) * cols] = piece.astype(
                        jnp.bfloat16
                    )

    tile = 256

    def partial(chunk, target):
        lefts, places = [], []
        for term in range(terms):
            src = order[term // local_terms, term % local_terms, target] - sec * sectors
            inside = jnp.logical_and(src >= 0, src < sectors)
            place = jnp.clip(src, 0, sectors - 1)
            gate = jnp.where(inside, 1.0, 0.0)
            block = lbuf[term // local_terms, term % local_terms, place]
            lefts.append((block.astype(jnp.float32) * gate).astype(jnp.bfloat16))
            places.append(place)
        lhs = jnp.concatenate(lefts, axis=1)
        for n in range(0, width, tile):
            rhs = jnp.concatenate(
                [rt[chunk, term, places[term], :, n:n + tile] for term in range(terms)], axis=0
            )
            acc[:, n:n + tile] = jnp.dot(lhs, rhs, preferred_element_type=jnp.float32)

    def hop(chunk, owner, part, landing, sems, to):
        return pltpu.make_async_remote_copy(
            src_ref=sendbuf.at[chunk, owner, part], dst_ref=landing.at[chunk, owner, part],
            send_sem=send_sems.at[chunk, owner, part], recv_sem=sems.at[chunk, owner, part],
            device_id={"sec": to}, device_id_type=MESH,
        )

    def pass_on(chunk, owner, part, inner, landing, sems, to):
        partial(chunk, owner * sectors + part)

        @pl.when(inner)
        def _():
            hop(chunk, owner, part, landing, sems, to).wait_recv()
            acc[...] += landing[chunk, owner, part].astype(jnp.float32)

        sendbuf[chunk, owner, part] = acc[...].astype(jnp.bfloat16)
        hop(chunk, owner, part, landing, sems, to).start()

    up = lax.rem(sec + 1, sec_count)
    down = lax.rem(sec + sec_count - 1, sec_count)

    for chunk in range(chunks):
        for part in range(sectors):
            if chunk == 0:
                wave_copies[part].wait()
            transform(chunk, part)
        if chunk == 0:
            own_right.wait()
        contract(chunk, mpo)
        if chunk == 0:
            @pl.when(rep == 0)
            def _():
                for copy in env_copies:
                    copy.wait_send()
                signal(turn, {"rep": 1})

            @pl.when(rep == 1)
            def _():
                pl.semaphore_wait(turn, 1)
                for copy in env_copies:
                    copy.start()

        for step in range(1, mpo_count):
            if chunk == 0:
                right_copies[step - 1].wait_recv()
            contract(chunk, lax.rem(mpo + mpo_count - step, mpo_count))
        if chunk == 0:
            own_left.wait()
            to_scalars.wait()
            for copy in left_copies:
                copy.wait_recv()

        @pl.loop(0, sec_count - 1)
        def _(step):
            above = sec + sec_count - 1 - step
            below = step - (sec_count - 1) + sec

            @pl.when(above < sec_count)
            def _():
                @pl.loop(0, sectors)
                def _(part):
                    pass_on(chunk, above, part, sec > 0, from_left, fl_sems, up)

            @pl.when(below >= 0)
            def _():
                @pl.loop(0, sectors)
                def _(part):
                    pass_on(chunk, below, part, sec < sec_count - 1, from_right, fr_sems, down)

    for chunk in range(chunks):
        for part in range(sectors):
            partial(chunk, sec * sectors + part)

            @pl.when(sec > 0)
            def _():
                hop(chunk, sec, part, from_left, fl_sems, up).wait_recv()
                acc[...] += from_left[chunk, sec, part].astype(jnp.float32)

            @pl.when(sec < sec_count - 1)
            def _():
                hop(chunk, sec, part, from_right, fr_sems, down).wait_recv()
                acc[...] += from_right[chunk, sec, part].astype(jnp.float32)

            live = row_index < rows_ref[sec * sectors + part]
            for q in range(q_chunk):
                piece = acc[:, q * cols:(q + 1) * cols]
                out_ref[part, :, chunk * q_chunk + q, :] = jnp.where(live, piece, 0.0)

    @pl.loop(0, sec_count)
    def _(owner):
        @pl.when(owner != sec)
        def _():
            for chunk in range(chunks):
                for part in range(sectors):
                    hop(chunk, owner, part, from_left, fl_sems, up).wait_send()

    @pl.when(rep == 1)
    def _():
        for copy in env_copies:
            copy.wait_send()


def per_device(sec_count, mpo_count, wave, left_env, right_env, phys_op, source, sector_rows):
    sectors, dl, phys_all, cols = wave.shape
    local_terms = phys_op.shape[0]
    terms = local_terms * mpo_count
    q_here = phys_all // mpo_count
    vmem = pl.BlockSpec(memory_space=pltpu.VMEM)
    smem = pl.BlockSpec(memory_space=pltpu.SMEM)
    chunks = 2 if q_here % 2 == 0 else 1
    q_chunk = q_here // chunks
    width = q_chunk * cols
    bf16 = jnp.bfloat16
    out = pl.pallas_call(
        functools.partial(kernel, sec_count, mpo_count, q_here),
        out_shape=jax.ShapeDtypeStruct((sectors, dl, q_here, cols), jnp.float32),
        in_specs=[vmem, smem, vmem, vmem, vmem, vmem],
        out_specs=vmem,
        scratch_shapes=[
            pltpu.VMEM((mpo_count,) + source.shape, jnp.int32),
            pltpu.SMEM((mpo_count,) + source.shape, jnp.int32),
            pltpu.VMEM((mpo_count,) + phys_op.shape, bf16),
            pltpu.VMEM((terms * q_here * GROUP, terms * phys_all), bf16),
            pltpu.VMEM((chunks, terms * q_chunk * GROUP, GROUP * phys_all), bf16),
            pltpu.VMEM((2, sectors, dl * phys_all, cols), bf16),
            pltpu.VMEM((mpo_count,) + left_env.shape, bf16),
            pltpu.VMEM((mpo_count,) + right_env.shape, bf16),
            pltpu.VMEM((sectors, terms * q_chunk, dl, 2 * cols), bf16),
            pltpu.VMEM((chunks, terms, sectors, dl, width), bf16),
            pltpu.VMEM((dl, width), jnp.float32),
            pltpu.VMEM((chunks, sec_count, sectors, dl, width), bf16),
            pltpu.VMEM((chunks, sec_count, sectors, dl, width), bf16),
            pltpu.VMEM((chunks, sec_count, sectors, dl, width), bf16),
            pltpu.SemaphoreType.DMA((2, sectors)),
            pltpu.SemaphoreType.DMA((2, 2, mpo_count)),
            pltpu.SemaphoreType.DMA((2, mpo_count)),
            pltpu.SemaphoreType.DMA((2, mpo_count)),
            pltpu.SemaphoreType.DMA((chunks, sec_count, sectors)),
            pltpu.SemaphoreType.DMA((chunks, sec_count, sectors)),
            pltpu.SemaphoreType.DMA((chunks, sec_count, sectors)),
            pltpu.SemaphoreType.DMA((4,)),
            pltpu.SemaphoreType.REGULAR,
        ],
        compiler_params=pltpu.CompilerParams(
            collective_id=0, has_side_effects=True, vmem_limit_bytes=56 * 1024 * 1024
        ),
        cost_estimate=pl.CostEstimate(
            flops=6 * 10**9, bytes_accessed=8 * 2**20, transcendentals=0
        ),
    )(
        source, sector_rows, wave.reshape(sectors, dl * phys_all, cols),
        left_env, right_env, phys_op,
    )
    return out


def solution(mesh):
    placed = (
        P(("groups", "sec"), None, None, "rep"),
        P(("groups", "mpo"), "sec", None, None),
        P(("groups", "mpo"), "sec", "rep", None),
        P(("groups", "mpo"), None, None),
        P(("groups", "mpo"), None),
        P("groups"),
    )
    return jax.shard_map(
        functools.partial(per_device, mesh.shape["sec"], mesh.shape["mpo"]),
        mesh=mesh,
        in_specs=placed,
        out_specs=P(("groups", "sec"), None, "mpo", "rep"),
        check_vma=False,
    )
```

```python
import functools

import jax
import jax.numpy as jnp
from jax import lax
from jax.experimental import pallas as pl
from jax.experimental.pallas import tpu as pltpu
from jax.sharding import PartitionSpec as P

MESH = pl.DeviceIdType.MESH
GROUP = 16


def split(value, size):
    if size & (size - 1):
        return value // size, value % size
    return lax.shift_right_logical(value, size.bit_length() - 1), value & (size - 1)


def signal(sem, where):
    pl.semaphore_signal(sem, inc=1, device_id=where, device_id_type=MESH)


def kernel(
    sec_count, mpo_count, q_here,
    source_ref, rows_ref, wave_ref, left_ref, right_ref, phys_ref,
    out_ref,
    order_buf, order, pbuf, pick_ref, op_ref, wbuf, lbuf, rbuf, ph, rt, acc, sendbuf, from_left, from_right,
    wave_sems, small_sems, left_sems, right_sems, send_sems, fl_sems, fr_sems, local_sems, turn,
):
    sec = lax.axis_index("sec")
    mpo = lax.axis_index("mpo")
    rep = lax.axis_index("rep")
    sectors, dl = left_ref.shape[1], left_ref.shape[2]
    local_terms = left_ref.shape[0]
    terms = local_terms * mpo_count
    cols = right_ref.shape[2]
    depth = wbuf.shape[2] // dl
    chunks = rt.shape[0]
    q_chunk = q_here // chunks
    width = q_chunk * cols

    barrier = pltpu.get_barrier_semaphore()
    signal(barrier, {"rep": 1 - rep})
    for step in range(1, mpo_count):
        signal(barrier, {"mpo": lax.rem(mpo + step, mpo_count)})

    @pl.when(sec > 0)
    def _():
        signal(barrier, {"sec": sec - 1})

    @pl.when(sec < sec_count - 1)
    def _():
        signal(barrier, {"sec": sec + 1})

    phys_all = phys_ref.shape[1]
    spread_rows = op_ref.shape[0] * op_ref.shape[1]
    spread_cols = op_ref.shape[2]
    r = lax.broadcasted_iota(jnp.int32, (spread_rows, 1), 0)
    c = lax.broadcasted_iota(jnp.int32, (1, terms * phys_all), 1)
    r, lane = split(r, GROUP)
    r, q_in = split(r, q_chunk)
    chunk_of, term_of = split(r, terms)
    want = term_of * phys_all + mpo * q_here + chunk_of * q_chunk + q_in
    pick_ref[...] = jnp.where(want == c, 1.0, 0.0).astype(jnp.bfloat16)
    c = lax.broadcasted_iota(jnp.int32, (1, spread_cols), 1)
    mask = jnp.where(lane == split(c, phys_all)[0], 1.0, 0.0).astype(jnp.bfloat16)
    op_ref[...] = mask.reshape(op_ref.shape)
    neighbours = (sec > 0).astype(jnp.int32) + (sec < sec_count - 1).astype(jnp.int32)
    pl.semaphore_wait(barrier, mpo_count + neighbours)

    wave_copies = [
        pltpu.make_async_remote_copy(
            src_ref=wave_ref.at[part], dst_ref=wbuf.at[rep, part],
            send_sem=wave_sems.at[0, part], recv_sem=wave_sems.at[1, part],
            device_id={"rep": 1 - rep}, device_id_type=MESH,
        )
        for part in range(sectors)
    ]

    def to_peers(ref, buf, sems):
        return [
            pltpu.make_async_remote_copy(
                src_ref=ref, dst_ref=buf.at[mpo],
                send_sem=sems.at[0, step], recv_sem=sems.at[1, step],
                device_id={"mpo": lax.rem(mpo + step, mpo_count)}, device_id_type=MESH,
            )
            for step in range(1, mpo_count)
        ]

    phys_copies = to_peers(phys_ref, pbuf, small_sems.at[0])
    order_copies = to_peers(source_ref, order_buf, small_sems.at[1])
    right_copies = to_peers(right_ref, rbuf, right_sems)
    left_copies = to_peers(left_ref, lbuf, left_sems)
    env_copies = right_copies + left_copies
    for copy in phys_copies + order_copies:
        copy.start()
    for copy in wave_copies:
        copy.start()

    @pl.when(rep == 0)
    def _():
        for copy in env_copies:
            copy.start()

    own_wave = pltpu.make_async_copy(wave_ref, wbuf.at[rep], local_sems.at[0])
    own_left = pltpu.make_async_copy(left_ref, lbuf.at[mpo], local_sems.at[1])
    own_right = pltpu.make_async_copy(right_ref, rbuf.at[mpo], local_sems.at[2])
    own_wave.start()
    own_left.start()
    own_right.start()
    pbuf[mpo] = phys_ref[...]
    order_buf[mpo] = source_ref[...]
    for copy in phys_copies + order_copies:
        copy.wait()
    to_scalars = pltpu.make_async_copy(order_buf, order, local_sems.at[3])
    to_scalars.start()
    flat = pbuf[...].reshape(terms * phys_all, phys_all)
    tall = jnp.dot(pick_ref[...], flat, preferred_element_type=jnp.float32).astype(jnp.bfloat16)
    p = lax.broadcasted_iota(jnp.int32, (phys_all, spread_cols), 0)
    c = lax.broadcasted_iota(jnp.int32, (phys_all, spread_cols), 1)
    repeat = jnp.where(split(c, phys_all)[1] == p, 1.0, 0.0).astype(jnp.bfloat16)
    wide = jnp.dot(tall, repeat, preferred_element_type=jnp.float32).reshape(op_ref.shape)
    op_ref[...] = jnp.where(op_ref[...].astype(jnp.float32) > 0.5, wide, 0.0).astype(jnp.bfloat16)
    own_wave.wait()

    def transform(chunk, part):
        @pl.loop(0, dl // GROUP, unroll=2)
        def _(group):
            rows = pl.ds(pl.multiple_of(group * (GROUP * depth), GROUP * depth), GROUP * depth)
            both = jnp.concatenate([wbuf[0, part, rows, :], wbuf[1, part, rows, :]], axis=1)
            result = jnp.dot(op_ref[chunk], both, preferred_element_type=jnp.float32)
            l_rows = pl.ds(pl.multiple_of(group * GROUP, GROUP), GROUP)
            ph[part, :, l_rows, :] = result.astype(jnp.bfloat16).reshape(
                terms * q_chunk, GROUP, 2 * cols
            )

    row_index = lax.broadcasted_iota(jnp.int32, (dl, cols), 0)

    def contract(chunk, owner):
        for part in range(sectors):
            live = row_index < rows_ref[sec * sectors + part]

            @pl.loop(0, local_terms, unroll=2)
            def _(term):
                whole_term = owner * local_terms + term
                states = ph[part, pl.ds(whole_term * q_chunk, q_chunk)]
                result = lax.dot_general(
                    states.reshape(q_chunk * dl, 2 * cols),
                    rbuf[owner, term, part],
                    (((1,), (1,)), ((), ())),
                    preferred_element_type=jnp.float32,
                )
                for q in range(q_chunk):
                    piece = jnp.where(live, result[q * dl:(q + 1) * dl], 0.0)
                    rt[chunk, whole_term, part, :, q * cols:(q + 1) * cols] = piece.astype(
                        jnp.bfloat16
                    )

    tile = min(256, width)

    def partial(chunk, target):
        lefts, places = [], []
        for term in range(terms):
            src = order[term // local_terms, term % local_terms, target] - sec * sectors
            inside = jnp.logical_and(src >= 0, src < sectors)
            place = jnp.clip(src, 0, sectors - 1)
            gate = jnp.where(inside, 1.0, 0.0)
            block = lbuf[term // local_terms, term % local_terms, place]
            lefts.append((block.astype(jnp.float32) * gate).astype(jnp.bfloat16))
            places.append(place)
        lhs = jnp.concatenate(lefts, axis=1)
        for n in range(0, width, tile):
            rhs = jnp.concatenate(
                [rt[chunk, term, places[term], :, n:n + tile] for term in range(terms)], axis=0
            )
            acc[:, n:n + tile] = jnp.dot(lhs, rhs, preferred_element_type=jnp.float32)

    def hop(chunk, owner, part, landing, sems, to):
        return pltpu.make_async_remote_copy(
            src_ref=sendbuf.at[chunk, owner, part], dst_ref=landing.at[chunk, owner, part],
            send_sem=send_sems.at[chunk, owner, part], recv_sem=sems.at[chunk, owner, part],
            device_id={"sec": to}, device_id_type=MESH,
        )

    def pass_on(chunk, owner, part, inner, landing, sems, to):
        partial(chunk, owner * sectors + part)

        @pl.when(inner)
        def _():
            hop(chunk, owner, part, landing, sems, to).wait_recv()
            acc[...] += landing[chunk, owner, part].astype(jnp.float32)

        sendbuf[chunk, owner, part] = acc[...].astype(jnp.bfloat16)
        hop(chunk, owner, part, landing, sems, to).start()

    up = lax.rem(sec + 1, sec_count)
    down = lax.rem(sec + sec_count - 1, sec_count)

    def one_chunk(chunk, first):
        for part in range(sectors):
            if first:
                wave_copies[part].wait()
            transform(chunk, part)
        if first:
            own_right.wait()
        contract(chunk, mpo)
        if first:
            @pl.when(rep == 0)
            def _():
                for copy in env_copies:
                    copy.wait_send()
                signal(turn, {"rep": 1})

            @pl.when(rep == 1)
            def _():
                pl.semaphore_wait(turn, 1)
                for copy in env_copies:
                    copy.start()

        for step in range(1, mpo_count):
            if first:
                right_copies[step - 1].wait_recv()
            contract(chunk, lax.rem(mpo + mpo_count - step, mpo_count))
        if first:
            own_left.wait()
            to_scalars.wait()
            for copy in left_copies:
                copy.wait_recv()

        @pl.loop(0, sec_count - 1)
        def _(step):
            above = sec + sec_count - 1 - step
            below = step - (sec_count - 1) + sec

            @pl.when(above < sec_count)
            def _():
                @pl.loop(0, sectors)
                def _(part):
                    pass_on(chunk, above, part, sec > 0, from_left, fl_sems, up)

            @pl.when(below >= 0)
            def _():
                @pl.loop(0, sectors)
                def _(part):
                    pass_on(chunk, below, part, sec < sec_count - 1, from_right, fr_sems, down)

    one_chunk(0, True)

    @pl.loop(1, chunks)
    def _(chunk):
        one_chunk(chunk, False)

    for chunk in range(chunks):
        for part in range(sectors):
            partial(chunk, sec * sectors + part)

            @pl.when(sec > 0)
            def _():
                hop(chunk, sec, part, from_left, fl_sems, up).wait_recv()
                acc[...] += from_left[chunk, sec, part].astype(jnp.float32)

            @pl.when(sec < sec_count - 1)
            def _():
                hop(chunk, sec, part, from_right, fr_sems, down).wait_recv()
                acc[...] += from_right[chunk, sec, part].astype(jnp.float32)

            live = row_index < rows_ref[sec * sectors + part]
            for q in range(q_chunk):
                piece = acc[:, q * cols:(q + 1) * cols]
                out_ref[part, :, chunk * q_chunk + q, :] = jnp.where(live, piece, 0.0)

    @pl.loop(0, sec_count)
    def _(owner):
        @pl.when(owner != sec)
        def _():
            for chunk in range(chunks):
                for part in range(sectors):
                    hop(chunk, owner, part, from_left, fl_sems, up).wait_send()

    @pl.when(rep == 1)
    def _():
        for copy in env_copies:
            copy.wait_send()


def per_device(sec_count, mpo_count, wave, left_env, right_env, phys_op, source, sector_rows):
    sectors, dl, phys_all, cols = wave.shape
    local_terms = phys_op.shape[0]
    terms = local_terms * mpo_count
    q_here = phys_all // mpo_count
    vmem = pl.BlockSpec(memory_space=pltpu.VMEM)
    smem = pl.BlockSpec(memory_space=pltpu.SMEM)
    chunks = 4 if q_here % 4 == 0 else 1
    q_chunk = q_here // chunks
    width = q_chunk * cols
    bf16 = jnp.bfloat16
    out = pl.pallas_call(
        functools.partial(kernel, sec_count, mpo_count, q_here),
        out_shape=jax.ShapeDtypeStruct((sectors, dl, q_here, cols), jnp.float32),
        in_specs=[vmem, smem, vmem, vmem, vmem, vmem],
        out_specs=vmem,
        scratch_shapes=[
            pltpu.VMEM((mpo_count,) + source.shape, jnp.int32),
            pltpu.SMEM((mpo_count,) + source.shape, jnp.int32),
            pltpu.VMEM((mpo_count,) + phys_op.shape, bf16),
            pltpu.VMEM((terms * q_here * GROUP, terms * phys_all), bf16),
            pltpu.VMEM((chunks, terms * q_chunk * GROUP, GROUP * phys_all), bf16),
            pltpu.VMEM((2, sectors, dl * phys_all, cols), bf16),
            pltpu.VMEM((mpo_count,) + left_env.shape, bf16),
            pltpu.VMEM((mpo_count,) + right_env.shape, bf16),
            pltpu.VMEM((sectors, terms * q_chunk, dl, 2 * cols), bf16),
            pltpu.VMEM((chunks, terms, sectors, dl, width), bf16),
            pltpu.VMEM((dl, width), jnp.float32),
            pltpu.VMEM((chunks, sec_count, sectors, dl, width), bf16),
            pltpu.VMEM((chunks, sec_count, sectors, dl, width), bf16),
            pltpu.VMEM((chunks, sec_count, sectors, dl, width), bf16),
            pltpu.SemaphoreType.DMA((2, sectors)),
            pltpu.SemaphoreType.DMA((2, 2, mpo_count)),
            pltpu.SemaphoreType.DMA((2, mpo_count)),
            pltpu.SemaphoreType.DMA((2, mpo_count)),
            pltpu.SemaphoreType.DMA((chunks, sec_count, sectors)),
            pltpu.SemaphoreType.DMA((chunks, sec_count, sectors)),
            pltpu.SemaphoreType.DMA((chunks, sec_count, sectors)),
            pltpu.SemaphoreType.DMA((4,)),
            pltpu.SemaphoreType.REGULAR,
        ],
        compiler_params=pltpu.CompilerParams(
            collective_id=0, has_side_effects=True, vmem_limit_bytes=56 * 1024 * 1024
        ),
        cost_estimate=pl.CostEstimate(
            flops=6 * 10**9, bytes_accessed=8 * 2**20, transcendentals=0
        ),
    )(
        source, sector_rows, wave.reshape(sectors, dl * phys_all, cols),
        left_env, right_env, phys_op,
    )
    return out


def solution(mesh):
    placed = (
        P(("groups", "sec"), None, None, "rep"),
        P(("groups", "mpo"), "sec", None, None),
        P(("groups", "mpo"), "sec", "rep", None),
        P(("groups", "mpo"), None, None),
        P(("groups", "mpo"), None),
        P("groups"),
    )
    return jax.shard_map(
        functools.partial(per_device, mesh.shape["sec"], mesh.shape["mpo"]),
        mesh=mesh,
        in_specs=placed,
        out_specs=P(("groups", "sec"), None, "mpo", "rep"),
        check_vma=False,
    )
```

```python
import functools

import jax
import jax.numpy as jnp
from jax import lax
from jax.experimental import pallas as pl
from jax.experimental.pallas import tpu as pltpu
from jax.sharding import PartitionSpec as P

MESH = pl.DeviceIdType.MESH
GROUP = 16


def split(value, size):
    if size & (size - 1):
        return value // size, value % size
    return lax.shift_right_logical(value, size.bit_length() - 1), value & (size - 1)


def signal(sem, where):
    pl.semaphore_signal(sem, inc=1, device_id=where, device_id_type=MESH)


def kernel(
    sec_count, mpo_count, q_here,
    source_ref, rows_ref, wave_ref, left_ref, right_ref, phys_ref,
    out_ref,
    order_buf, order, pbuf, pick_ref, op_ref, wbuf, lbuf, rbuf, ph, rt, acc, sendbuf, from_left, from_right,
    wave_sems, small_sems, left_sems, right_sems, send_sems, fl_sems, fr_sems, local_sems, turn,
):
    sec = lax.axis_index("sec")
    mpo = lax.axis_index("mpo")
    rep = lax.axis_index("rep")
    sectors, dl = left_ref.shape[1], left_ref.shape[2]
    local_terms = left_ref.shape[0]
    terms = local_terms * mpo_count
    cols = right_ref.shape[2]
    depth = wbuf.shape[2] // dl
    chunks = rt.shape[0]
    q_chunk = q_here // chunks
    width = q_chunk * cols

    barrier = pltpu.get_barrier_semaphore()
    signal(barrier, {"rep": 1 - rep})
    for step in range(1, mpo_count):
        signal(barrier, {"mpo": lax.rem(mpo + step, mpo_count)})

    @pl.when(sec > 0)
    def _():
        signal(barrier, {"sec": sec - 1})

    @pl.when(sec < sec_count - 1)
    def _():
        signal(barrier, {"sec": sec + 1})

    phys_all = phys_ref.shape[1]
    spread_rows = op_ref.shape[0] * op_ref.shape[1]
    spread_cols = op_ref.shape[2]
    r = lax.broadcasted_iota(jnp.int32, (spread_rows, 1), 0)
    c = lax.broadcasted_iota(jnp.int32, (1, terms * phys_all), 1)
    r, lane = split(r, GROUP)
    r, q_in = split(r, q_chunk)
    chunk_of, term_of = split(r, terms)
    want = term_of * phys_all + mpo * q_here + chunk_of * q_chunk + q_in
    pick_ref[...] = jnp.where(want == c, 1.0, 0.0).astype(jnp.bfloat16)
    c = lax.broadcasted_iota(jnp.int32, (1, spread_cols), 1)
    mask = jnp.where(lane == split(c, phys_all)[0], 1.0, 0.0).astype(jnp.bfloat16)
    op_ref[...] = mask.reshape(op_ref.shape)
    neighbours = (sec > 0).astype(jnp.int32) + (sec < sec_count - 1).astype(jnp.int32)
    pl.semaphore_wait(barrier, mpo_count + neighbours)

    wave_copies = [
        pltpu.make_async_remote_copy(
            src_ref=wave_ref.at[part], dst_ref=wbuf.at[rep, part],
            send_sem=wave_sems.at[0, part], recv_sem=wave_sems.at[1, part],
            device_id={"rep": 1 - rep}, device_id_type=MESH,
        )
        for part in range(sectors)
    ]

    def to_peers(ref, buf, sems):
        return [
            pltpu.make_async_remote_copy(
                src_ref=ref, dst_ref=buf.at[mpo],
                send_sem=sems.at[0, step], recv_sem=sems.at[1, step],
                device_id={"mpo": lax.rem(mpo + step, mpo_count)}, device_id_type=MESH,
            )
            for step in range(1, mpo_count)
        ]

    phys_copies = to_peers(phys_ref, pbuf, small_sems.at[0])
    order_copies = to_peers(source_ref, order_buf, small_sems.at[1])
    right_copies = to_peers(right_ref, rbuf, right_sems)
    left_copies = to_peers(left_ref, lbuf, left_sems)
    env_copies = right_copies + left_copies
    for copy in phys_copies + order_copies:
        copy.start()
    for copy in wave_copies:
        copy.start()

    @pl.when(rep == 0)
    def _():
        for copy in env_copies:
            copy.start()

    own_wave = pltpu.make_async_copy(wave_ref, wbuf.at[rep], local_sems.at[0])
    own_left = pltpu.make_async_copy(left_ref, lbuf.at[mpo], local_sems.at[1])
    own_right = pltpu.make_async_copy(right_ref, rbuf.at[mpo], local_sems.at[2])
    own_wave.start()
    own_left.start()
    own_right.start()
    pbuf[mpo] = phys_ref[...]
    order_buf[mpo] = source_ref[...]
    for copy in phys_copies + order_copies:
        copy.wait()
    to_scalars = pltpu.make_async_copy(order_buf, order, local_sems.at[3])
    to_scalars.start()
    flat = pbuf[...].reshape(terms * phys_all, phys_all)
    tall = jnp.dot(pick_ref[...], flat, preferred_element_type=jnp.float32).astype(jnp.bfloat16)
    p = lax.broadcasted_iota(jnp.int32, (phys_all, spread_cols), 0)
    c = lax.broadcasted_iota(jnp.int32, (phys_all, spread_cols), 1)
    repeat = jnp.where(split(c, phys_all)[1] == p, 1.0, 0.0).astype(jnp.bfloat16)
    wide = jnp.dot(tall, repeat, preferred_element_type=jnp.float32).reshape(op_ref.shape)
    op_ref[...] = jnp.where(op_ref[...].astype(jnp.float32) > 0.5, wide, 0.0).astype(jnp.bfloat16)
    own_wave.wait()

    def transform(chunk, part):
        @pl.loop(0, dl // GROUP, unroll=2)
        def _(group):
            rows = pl.ds(pl.multiple_of(group * (GROUP * depth), GROUP * depth), GROUP * depth)
            both = jnp.concatenate([wbuf[0, part, rows, :], wbuf[1, part, rows, :]], axis=1)
            result = jnp.dot(op_ref[chunk], both, preferred_element_type=jnp.float32)
            l_rows = pl.ds(pl.multiple_of(group * GROUP, GROUP), GROUP)
            ph[part, :, l_rows, :] = result.astype(jnp.bfloat16).reshape(
                terms * q_chunk, GROUP, 2 * cols
            )

    row_index = lax.broadcasted_iota(jnp.int32, (dl, cols), 0)

    def contract(chunk, owner):
        for part in range(sectors):
            live = row_index < rows_ref[sec * sectors + part]

            @pl.loop(0, local_terms, unroll=2)
            def _(term):
                whole_term = owner * local_terms + term
                states = ph[part, pl.ds(whole_term * q_chunk, q_chunk)]
                result = lax.dot_general(
                    states.reshape(q_chunk * dl, 2 * cols),
                    rbuf[owner, term, part],
                    (((1,), (1,)), ((), ())),
                    preferred_element_type=jnp.float32,
                )
                for q in range(q_chunk):
                    piece = jnp.where(live, result[q * dl:(q + 1) * dl], 0.0)
                    rt[chunk, whole_term, part, :, q * cols:(q + 1) * cols] = piece.astype(
                        jnp.bfloat16
                    )

    tile = 256

    def partial(chunk, target):
        lefts, places = [], []
        for term in range(terms):
            src = order[term // local_terms, term % local_terms, target] - sec * sectors
            inside = jnp.logical_and(src >= 0, src < sectors)
            place = jnp.clip(src, 0, sectors - 1)
            gate = jnp.where(inside, 1.0, 0.0)
            block = lbuf[term // local_terms, term % local_terms, place]
            lefts.append((block.astype(jnp.float32) * gate).astype(jnp.bfloat16))
            places.append(place)
        lhs = jnp.concatenate(lefts, axis=1)
        for n in range(0, width, tile):
            rhs = jnp.concatenate(
                [rt[chunk, term, places[term], :, n:n + tile] for term in range(terms)], axis=0
            )
            acc[:, n:n + tile] = jnp.dot(lhs, rhs, preferred_element_type=jnp.float32)

    def hop(chunk, owner, part, landing, sems, to):
        return pltpu.make_async_remote_copy(
            src_ref=sendbuf.at[chunk, owner, part], dst_ref=landing.at[chunk, owner, part],
            send_sem=send_sems.at[chunk, owner, part], recv_sem=sems.at[chunk, owner, part],
            device_id={"sec": to}, device_id_type=MESH,
        )

    def pass_on(chunk, owner, part, inner, landing, sems, to):
        partial(chunk, owner * sectors + part)

        @pl.when(inner)
        def _():
            hop(chunk, owner, part, landing, sems, to).wait_recv()
            acc[...] += landing[chunk, owner, part].astype(jnp.float32)

        sendbuf[chunk, owner, part] = acc[...].astype(jnp.bfloat16)
        hop(chunk, owner, part, landing, sems, to).start()

    up = lax.rem(sec + 1, sec_count)
    down = lax.rem(sec + sec_count - 1, sec_count)

    def build(chunk):
        for part in range(sectors):
            if chunk == 0:
                wave_copies[part].wait()
            transform(chunk, part)
        if chunk == 0:
            own_right.wait()
        contract(chunk, mpo)
        if chunk == 0:
            @pl.when(rep == 0)
            def _():
                for copy in env_copies:
                    copy.wait_send()
                signal(turn, {"rep": 1})

            @pl.when(rep == 1)
            def _():
                pl.semaphore_wait(turn, 1)
                for copy in env_copies:
                    copy.start()

        for step in range(1, mpo_count):
            if chunk == 0:
                right_copies[step - 1].wait_recv()
            contract(chunk, lax.rem(mpo + mpo_count - step, mpo_count))
        if chunk == 0:
            own_left.wait()
            to_scalars.wait()
            for copy in left_copies:
                copy.wait_recv()

    def send(chunk):
        @pl.loop(0, sec_count - 1)
        def _(step):
            above = sec + sec_count - 1 - step
            below = step - (sec_count - 1) + sec

            @pl.when(above < sec_count)
            def _():
                @pl.loop(0, sectors)
                def _(part):
                    pass_on(chunk, above, part, sec > 0, from_left, fl_sems, up)

            @pl.when(below >= 0)
            def _():
                @pl.loop(0, sectors)
                def _(part):
                    pass_on(chunk, below, part, sec < sec_count - 1, from_right, fr_sems, down)

    at_end = jnp.logical_or(sec == 0, sec == sec_count - 1)
    build(0)
    for chunk in range(chunks):
        if chunk + 1 < chunks:
            @pl.when(jnp.logical_not(at_end))
            def _():
                build(chunk + 1)

        send(chunk)
        if chunk + 1 < chunks:
            @pl.when(at_end)
            def _():
                build(chunk + 1)

    for chunk in range(chunks):
        for part in range(sectors):
            partial(chunk, sec * sectors + part)

            @pl.when(sec > 0)
            def _():
                hop(chunk, sec, part, from_left, fl_sems, up).wait_recv()
                acc[...] += from_left[chunk, sec, part].astype(jnp.float32)

            @pl.when(sec < sec_count - 1)
            def _():
                hop(chunk, sec, part, from_right, fr_sems, down).wait_recv()
                acc[...] += from_right[chunk, sec, part].astype(jnp.float32)

            live = row_index < rows_ref[sec * sectors + part]
            for q in range(q_chunk):
                piece = acc[:, q * cols:(q + 1) * cols]
                out_ref[part, :, chunk * q_chunk + q, :] = jnp.where(live, piece, 0.0)

    @pl.loop(0, sec_count)
    def _(owner):
        @pl.when(owner != sec)
        def _():
            for chunk in range(chunks):
                for part in range(sectors):
                    hop(chunk, owner, part, from_left, fl_sems, up).wait_send()

    @pl.when(rep == 1)
    def _():
        for copy in env_copies:
            copy.wait_send()


def per_device(sec_count, mpo_count, wave, left_env, right_env, phys_op, source, sector_rows):
    sectors, dl, phys_all, cols = wave.shape
    local_terms = phys_op.shape[0]
    terms = local_terms * mpo_count
    q_here = phys_all // mpo_count
    vmem = pl.BlockSpec(memory_space=pltpu.VMEM)
    smem = pl.BlockSpec(memory_space=pltpu.SMEM)
    chunks = 2 if q_here % 2 == 0 else 1
    q_chunk = q_here // chunks
    width = q_chunk * cols
    bf16 = jnp.bfloat16
    out = pl.pallas_call(
        functools.partial(kernel, sec_count, mpo_count, q_here),
        out_shape=jax.ShapeDtypeStruct((sectors, dl, q_here, cols), jnp.float32),
        in_specs=[vmem, smem, vmem, vmem, vmem, vmem],
        out_specs=vmem,
        scratch_shapes=[
            pltpu.VMEM((mpo_count,) + source.shape, jnp.int32),
            pltpu.SMEM((mpo_count,) + source.shape, jnp.int32),
            pltpu.VMEM((mpo_count,) + phys_op.shape, bf16),
            pltpu.VMEM((terms * q_here * GROUP, terms * phys_all), bf16),
            pltpu.VMEM((chunks, terms * q_chunk * GROUP, GROUP * phys_all), bf16),
            pltpu.VMEM((2, sectors, dl * phys_all, cols), bf16),
            pltpu.VMEM((mpo_count,) + left_env.shape, bf16),
            pltpu.VMEM((mpo_count,) + right_env.shape, bf16),
            pltpu.VMEM((sectors, terms * q_chunk, dl, 2 * cols), bf16),
            pltpu.VMEM((chunks, terms, sectors, dl, width), bf16),
            pltpu.VMEM((dl, width), jnp.float32),
            pltpu.VMEM((chunks, sec_count, sectors, dl, width), bf16),
            pltpu.VMEM((chunks, sec_count, sectors, dl, width), bf16),
            pltpu.VMEM((chunks, sec_count, sectors, dl, width), bf16),
            pltpu.SemaphoreType.DMA((2, sectors)),
            pltpu.SemaphoreType.DMA((2, 2, mpo_count)),
            pltpu.SemaphoreType.DMA((2, mpo_count)),
            pltpu.SemaphoreType.DMA((2, mpo_count)),
            pltpu.SemaphoreType.DMA((chunks, sec_count, sectors)),
            pltpu.SemaphoreType.DMA((chunks, sec_count, sectors)),
            pltpu.SemaphoreType.DMA((chunks, sec_count, sectors)),
            pltpu.SemaphoreType.DMA((4,)),
            pltpu.SemaphoreType.REGULAR,
        ],
        compiler_params=pltpu.CompilerParams(
            collective_id=0, has_side_effects=True, vmem_limit_bytes=56 * 1024 * 1024
        ),
        cost_estimate=pl.CostEstimate(
            flops=6 * 10**9, bytes_accessed=8 * 2**20, transcendentals=0
        ),
    )(
        source, sector_rows, wave.reshape(sectors, dl * phys_all, cols),
        left_env, right_env, phys_op,
    )
    return out


def solution(mesh):
    placed = (
        P(("groups", "sec"), None, None, "rep"),
        P(("groups", "mpo"), "sec", None, None),
        P(("groups", "mpo"), "sec", "rep", None),
        P(("groups", "mpo"), None, None),
        P(("groups", "mpo"), None),
        P("groups"),
    )
    return jax.shard_map(
        functools.partial(per_device, mesh.shape["sec"], mesh.shape["mpo"]),
        mesh=mesh,
        in_specs=placed,
        out_specs=P(("groups", "sec"), None, "mpo", "rep"),
        check_vma=False,
    )
```
